128 devices in a mesh: row: 8 (over x_lo, z), col: 16 (over y, x_hi, core).
Axes of the slice: x: 4 (x_hi: 2, x_lo: 2; x = x_hi * 2 + x_lo), y: 4, z: 4, core: 2. Of those that a mesh axis runs over, the one named last changes fastest.
Arguments:
- start_vectors: bfloat16 [65536, 512], P(('row', 'col')), may hold values from -6 to 6
- tiles: bfloat16 [512, 16, 2, 128, 128], P('row', 'col'), may hold values from -0.046875 to 0.046875
- tile_col: int32 [512, 16, 2], P('row', 'col'), may hold values from 0 to 31, as said below
- tile_count: int32 [512, 16], P('row', 'col'), may hold values from 1 to 2, as said below
Outputs:
- filtered: bfloat16 [65536, 512], P(('row', 'col'))
The draws below stay inside these ranges and needn't reach their ends.
Inputs may be any that keep to these rules, and one draw needn't show every extreme that they name: `tile_col`: the 2 entries of one block row and one column group are distinct; every device's first block row uses local block columns 0 and 31. `tile_count`: every device's first block row has all 2 slots live in every column group.
All inputs are finite; a program needn't handle non-finite values.
Results may differ from the reference program's by a relative error of at most 0.019.
Values may be sent and summed in bfloat16 or wider, within the bound.
No kernel may reach another device: no remote copies, remote signals or barrier semaphores. Data moves between devices by JAX's collectives and lax.ppermute only.
A program may use at most 128 MiB of HBM per device.

```python
import jax
import jax.numpy as jnp
from jax import lax

BLK = 128
NV = 512
DEGREE = 3
BPD = 4
KR = 2
NB = 512
N = 65536
BR = 64
BC = 32
N_COL = 16


def draw_tile_col(key, part):
    key = jax.random.fold_in(key, 11)
    scores = jax.random.randint(key, (NB, N_COL, BC), 0, 1 << 20)
    position = jnp.arange(BC, dtype=jnp.int32)
    scores = scores * BC + position
    first_row = (jnp.arange(NB, dtype=jnp.int32) % BR == 0)[:, None, None]
    scores = jnp.where(first_row & (position == BC - 1), -2, scores)
    scores = jnp.where(first_row & (position == 0), -1, scores)
    ranked = jnp.argsort(scores, axis=-1)
    return ranked[..., :KR].astype(jnp.int32)


def draw_tile_count(key, part):
    key = jax.random.fold_in(key, 23)
    counts = jax.random.randint(key, (NB, N_COL), 1, KR + 1)
    first_row = (jnp.arange(NB, dtype=jnp.int32) % BR == 0)[:, None]
    return jnp.where(first_row, KR, counts).astype(jnp.int32)


def block_levels(own_key, shape, cuts, low, high):
    factor_of, own = 1.0, jax.random.fold_in(own_key, 6)
    for axis_at, blocks in cuts:
        steps = jnp.exp(jax.random.uniform(jax.random.fold_in(own, axis_at), (blocks,), jnp.float32, low / len(cuts), high / len(cuts)))
        factor_of = factor_of * jnp.repeat(steps, shape[axis_at] // blocks).reshape([-1 if axis == axis_at else 1 for axis in range(len(shape))])
    return factor_of


def gaussian(key, dims, scale, limit, pieces=(), kind=jnp.bfloat16):
    factor_of = block_levels(key, dims, pieces, -0.22, 0.18) if pieces else 1.0
    entries = jax.random.normal(key, dims, jnp.float32) * scale * factor_of
    return jnp.minimum(jnp.maximum(entries, -limit), limit).astype(kind)


def setup_inputs(seed: int = 0) -> dict:
    splits = jax.random.split(jax.random.key(seed), 5)
    start_vectors = gaussian(splits[0], (N, NV), 1.0, 6.0, ((0, 128),))
    tiles = gaussian(splits[1], (NB, N_COL, KR, BLK, BLK), (4 * KR * N_COL * BLK) ** -0.5, 0.046875, ((0, 8), (1, 16)))
    tile_col = draw_tile_col(jax.random.fold_in(splits[4], 71), 0)
    tile_count = draw_tile_count(jax.random.fold_in(splits[4], 71), 0)
    return dict(start_vectors=start_vectors, tiles=tiles, tile_col=tile_col, tile_count=tile_count)


def reference(start_vectors, tiles, tile_col, tile_count):
    live_slots = jnp.arange(KR, dtype=jnp.int32)[None, None, :] < tile_count[:, :, None]
    masked = jnp.where(live_slots[..., None, None], tiles, jnp.zeros((), tiles.dtype))
    group_ids = jnp.arange(N_COL, dtype=jnp.int32)[None, :, None]
    global_col = (((tile_col // BPD) * N_COL + group_ids) * BPD + tile_col % BPD).astype(jnp.int32)

    def apply_matrix(vectors):
        blocks = vectors.reshape(NB, BLK, NV)

        def one_row(row_item):
            row_tiles, row_cols = row_item
            picked = blocks[row_cols].astype(jnp.float32)
            group_sums = jnp.einsum("ckij,ckjn->cin", row_tiles.astype(jnp.float32), picked,
                                    precision=lax.Precision.HIGHEST)
            rounded = lax.optimization_barrier(group_sums.astype(jnp.bfloat16))
            return jnp.sum(rounded.astype(jnp.float32), axis=0)

        return lax.map(one_row, (masked, global_col)).reshape(NB * BLK, NV)

    previous = start_vectors
    current = apply_matrix(previous).astype(jnp.bfloat16)
    for degree in range(1, DEGREE):
        block_total = apply_matrix(current)
        following = (2.0 * block_total - previous.astype(jnp.float32)).astype(jnp.bfloat16)
        previous, current = current, following
    return current
```

```python
import functools

import jax
import jax.numpy as jnp
import numpy as np
from jax import lax
from jax.experimental import pallas as pl
from jax.experimental.pallas import tpu as pltpu
from jax.sharding import Mesh, PartitionSpec as P

DEGREE = 3
BLK = 128
LANES = 128
CHUNKS = 2
UNIT = 8
ROUTES = (
    ((2, 0, 0), (2, 1, 0)),
    ((2, 0, 1), (2, 1, 1)),
    ((1, 1, 0), (1, 1, 1)),
    ((3, 1, 0), (3, 1, 1)),
    ((1, 0, 0), (1, 0, 1)),
    ((3, 0, 0), (3, 0, 1)),
    ((0, 1, 0), (0, 1, 1)),
    ((0, 0, 0), (0, 0, 1)),
)


def ring(size, step):
    return [(i, (i + step) % size) for i in range(size)]


def swap(x, axis):
    return lax.ppermute(x, axis, [(0, 1), (1, 0)])


def product_kernel(order, picks, own_a, own_b, other_a, other_b, *refs):
    pieces, out, held = refs[:8], refs[8], refs[9]
    step = pl.program_id(0)

    @pl.when(step == 0)
    def _():
        for i, piece in enumerate(pieces):
            held[pl.ds(i * UNIT * BLK, UNIT * BLK), :] = piece[...]
        held[pl.ds(8 * UNIT * BLK, BLK), :] = jnp.zeros((BLK, LANES), held.dtype)

    for half, (own, other) in enumerate(((own_a, other_a), (own_b, other_b))):
        group = order[2 * step + half]
        for j in range(4):
            base = (group * 4 + j) * 4
            picked = jnp.concatenate(
                [held[pl.ds(pl.multiple_of(picks[base + k], BLK), BLK), :] for k in range(4)], axis=0
            )
            row = jnp.concatenate([own[j, 0], own[j, 1], other[j, 0], other[j, 1]], axis=1)
            total = jnp.dot(row, picked, preferred_element_type=jnp.float32)
            out[pl.ds((half * 4 + j) * BLK, BLK), :] = total.astype(out.dtype)


def products(order, picks, own, other, pieces):
    def tile_spec(half):
        return pl.BlockSpec((4, 2, BLK, BLK), lambda s, order, picks: (order[2 * s + half], 0, 0, 0))

    piece_spec = pl.BlockSpec((UNIT * BLK, LANES), lambda s, order, picks: (0, 0))
    return pl.pallas_call(
        product_kernel,
        grid_spec=pltpu.PrefetchScalarGridSpec(
            num_scalar_prefetch=2,
            grid=(8,),
            in_specs=[tile_spec(0), tile_spec(1), tile_spec(0), tile_spec(1)] + [piece_spec] * 8,
            out_specs=pl.BlockSpec((UNIT * BLK, LANES), lambda s, order, picks: (s, 0)),
            scratch_shapes=[pltpu.VMEM(((8 * UNIT + 1) * BLK, LANES), jnp.bfloat16)],
        ),
        out_shape=jax.ShapeDtypeStruct((8 * UNIT * BLK, LANES), jnp.bfloat16),
        compiler_params=pltpu.CompilerParams(vmem_limit_bytes=24 << 20),
        cost_estimate=pl.CostEstimate(flops=64 * 2 * 128 * 512 * 128, bytes_accessed=12 << 20, transcendentals=0),
        name="products",
    )(order, picks, own, own, other, other, *pieces)


def add(*terms):
    total = terms[0].astype(jnp.float32)
    for term in terms[1:]:
        total = total + term.astype(jnp.float32)
    return total


def body(start_vectors, tiles, tile_col, tile_count):
    xl, z, y, xh, c = (lax.axis_index(a) for a in ("xl", "z", "y", "xh", "c"))
    rows = start_vectors.shape[0]
    half = start_vectors.shape[1] // 2

    mine = lax.dynamic_slice(start_vectors, (0, c * half), (rows, half))
    theirs = swap(lax.dynamic_slice(start_vectors, (0, (1 - c) * half), (rows, half)), "c")
    first = [
        jnp.concatenate([part[:, i * LANES : (i + 1) * LANES] for part in (mine, theirs)], axis=0)
        for i in range(CHUNKS)
    ]

    own = tiles[:, 0]
    other = swap(own, "c")

    r, i = tile_col[:, 0] // 4, tile_col[:, 0] % 4
    dx, dz = (r // 4) ^ xl, (r - z) & 3
    at = jnp.where(dx == 0, jnp.where(dz == 0, 0, jnp.where(dz == 3, 1, 2)), jnp.where(dz == 0, 3, jnp.where(dz == 3, 4, 5)))
    far = dz == 2
    live = jnp.arange(2, dtype=jnp.int32)[None, :] < tile_count
    code_own = jnp.where(live, jnp.where(far, 48 + dx * 4, at * 8) + i, 64) * BLK
    code_other = jnp.where(live, jnp.where(far, 56 + dx * 4, at * 8 + 4) + i, 64) * BLK
    picks = jnp.concatenate([code_own, swap(code_other, "c")], axis=1).reshape(-1)

    routes = np.array(ROUTES, np.int32).reshape(16, 3)
    unit = ((y + routes[:, 0]) & 3) * 2 + (xh ^ routes[:, 1])
    order = (unit * 2 + (c ^ routes[:, 2])).astype(jnp.int32)

    def gather(v):
        h = v.shape[0] // 2
        up, down = ring(4, 1), ring(4, 3)
        from_up, from_down, across = lax.ppermute(v, "z", up), lax.ppermute(v, "z", down), swap(v, "xl")
        a_up, a_down = lax.ppermute(across, "z", up), lax.ppermute(across, "z", down)
        far_up = lax.ppermute(jnp.concatenate([from_up[:h], a_up[:h]], axis=0), "z", up)
        far_down = lax.ppermute(jnp.concatenate([from_down[h:], a_down[h:]], axis=0), "z", down)
        return v, from_up, from_down, across, a_up, a_down, far_up, far_down

    def scatter(p):
        u = UNIT * BLK
        h = u // 2
        p = [p[k * u : (k + 1) * u] for k in range(8)]
        up, down = ring(4, 1), ring(4, 3)
        got_up, got_down = lax.ppermute(p[0], "y", up), lax.ppermute(p[1], "y", down)

        def first_half(a, b):
            return jnp.concatenate([add(a[:h], b).astype(a.dtype), a[h:]], axis=0)

        def last_half(a, b):
            return jnp.concatenate([a[:h], add(a[h:], b).astype(a.dtype)], axis=0)

        x_up = lax.ppermute(first_half(p[2], got_up[h:]), "y", up)
        x_down = lax.ppermute(last_half(p[3], got_down[h:]), "y", down)
        n_up = lax.ppermute(first_half(p[4], got_up[:h]), "y", up)
        n_down = lax.ppermute(last_half(p[5], got_down[:h]), "y", down)
        crossed = swap(add(p[6], x_up, x_down).astype(p[6].dtype), "xh")
        return add(p[7], n_up, n_down, crossed)

    previous, current = [None] * CHUNKS, first
    for degree in range(DEGREE):
        following = []
        for k in range(CHUNKS):
            total = scatter(products(order, picks, own, other, gather(current[k])))
            if degree:
                total = 2.0 * total - previous[k].astype(jnp.float32)
            following.append(total.astype(jnp.bfloat16))
        previous, current = current, following

    kept = jnp.concatenate([v[:rows] for v in current], axis=1)
    got = swap(jnp.concatenate([v[rows:] for v in current], axis=1), "c")
    return jnp.where(c == 0, jnp.concatenate([kept, got], axis=1), jnp.concatenate([got, kept], axis=1))


def solution(mesh):
    axes = ("xl", "z", "y", "xh", "c")
    fine = Mesh(mesh.devices.reshape(2, 4, 4, 2, 2), axes)
    row, col = axes[:2], axes[2:]
    placed = (
        P(axes, None),
        P(row, col, None, None, None),
        P(row, col, None),
        P(row, col),
    )
    return jax.shard_map(body, mesh=fine, in_specs=placed, out_specs=P(axes, None), check_vma=False)
```

```python
import functools

import jax
import jax.numpy as jnp
import numpy as np
from jax import lax
from jax.experimental import pallas as pl
from jax.experimental.pallas import tpu as pltpu
from jax.sharding import Mesh, PartitionSpec as P

DEGREE = 3
BLK = 128
LANES = 128
CHUNKS = 2
UNIT = 8


def flips(first):
    return [(2 * i + c, 2 * (i ^ (1 if (c == 0) == first else 3)) + c) for i in range(4) for c in range(2)]


def swap(x, axis):
    return lax.ppermute(x, axis, [(0, 1), (1, 0)])


def product_kernel(order, picks, own_a, own_b, other_a, other_b, *refs):
    *pieces, out, held = refs
    step = pl.program_id(0)

    @pl.when(step == 0)
    def _():
        at = 0
        for piece in pieces:
            held[pl.ds(at, piece.shape[0]), :] = piece[...]
            at += piece.shape[0]
        held[pl.ds(8 * UNIT * BLK, BLK), :] = jnp.zeros((BLK, LANES), held.dtype)

    for half, (own, other) in enumerate(((own_a, other_a), (own_b, other_b))):
        group = order[2 * step + half]
        for j in range(4):
            base = (group * 4 + j) * 4
            picked = jnp.concatenate(
                [held[pl.ds(pl.multiple_of(picks[base + k], BLK), BLK), :] for k in range(4)], axis=0
            )
            row = jnp.concatenate([own[j, 0], own[j, 1], other[j, 0], other[j, 1]], axis=1)
            total = jnp.dot(row, picked, preferred_element_type=jnp.float32)
            out[pl.ds((half * 4 + j) * BLK, BLK), :] = total.astype(out.dtype)


def products(order, picks, own, other, pieces):
    def tile_spec(half):
        return pl.BlockSpec((4, 2, BLK, BLK), lambda s, order, picks: (order[2 * s + half], 0, 0, 0))

    return pl.pallas_call(
        product_kernel,
        grid_spec=pltpu.PrefetchScalarGridSpec(
            num_scalar_prefetch=2,
            grid=(8,),
            in_specs=[tile_spec(0), tile_spec(1), tile_spec(0), tile_spec(1)] + [pl.BlockSpec(piece.shape, lambda s, order, picks: (0, 0)) for piece in pieces],
            out_specs=pl.BlockSpec((UNIT * BLK, LANES), lambda s, order, picks: (s, 0)),
            scratch_shapes=[pltpu.VMEM(((8 * UNIT + 1) * BLK, LANES), jnp.bfloat16)],
        ),
        out_shape=jax.ShapeDtypeStruct((8 * UNIT * BLK, LANES), jnp.bfloat16),
        compiler_params=pltpu.CompilerParams(vmem_limit_bytes=24 << 20),
        cost_estimate=pl.CostEstimate(flops=64 * 2 * 128 * 512 * 128, bytes_accessed=12 << 20, transcendentals=0),
        name="products",
    )(order, picks, own, own, other, other, *pieces)


def add(*terms):
    total = terms[0].astype(jnp.float32)
    for term in terms[1:]:
        total = total + term.astype(jnp.float32)
    return total


def body(start_vectors, tiles, tile_col, tile_count):
    xl, z, y, xh, c = (lax.axis_index(a) for a in ("xl", "z", "y", "xh", "c"))
    rows = start_vectors.shape[0]
    half = start_vectors.shape[1] // 2

    mine = lax.dynamic_slice(start_vectors, (0, c * half), (rows, half))
    theirs = swap(lax.dynamic_slice(start_vectors, (0, (1 - c) * half), (rows, half)), "c")
    first = [
        jnp.concatenate([part[:, i * LANES : (i + 1) * LANES] for part in (mine, theirs)], axis=0)
        for i in range(CHUNKS)
    ]

    own = tiles[:, 0]
    other = swap(own, "c")

    r, i = tile_col[:, 0] // 4, tile_col[:, 0] % 4
    dx, dz = (r // 4) ^ xl, (r & 3) ^ z
    live = jnp.arange(2, dtype=jnp.int32)[None, :] < tile_count

    def code(core, shift):
        slot = jnp.where(dz == 0, 0, jnp.where(dz == 2, 3, jnp.where(dz == 1 + 2 * core, 1, 2)))
        return jnp.where(live, (slot * 2 + dx) * UNIT + shift + i, 8 * UNIT) * BLK

    picks = jnp.concatenate([code(c, 0), swap(code(1 - c, 4), "c")], axis=1).reshape(-1)

    far, near = 3 - 2 * c, 1 + 2 * c
    dy = jnp.stack([far, far, jnp.int32(2), jnp.int32(2), near, near, jnp.int32(0), jnp.int32(0)])
    unit = (y ^ dy) * 2 + (xh ^ np.array([1, 0] * 4, np.int32))
    order = ((unit * 2)[:, None] + (c ^ np.array([[0, 1]], np.int32))).reshape(-1).astype(jnp.int32)

    def gather(v):
        pair = jnp.concatenate([v, swap(v, "xl")], axis=0)
        side = lax.ppermute(pair, ("z", "c"), flips(True))
        rest = lax.ppermute(jnp.concatenate([pair, side], axis=0), ("z", "c"), flips(False))
        return pair, side, rest

    def scatter(p):
        u = UNIT * BLK
        one = lax.ppermute(p[: 4 * u], ("y", "c"), flips(False))
        two = lax.ppermute(add(p[4 * u : 6 * u], one[2 * u :]).astype(p.dtype), ("y", "c"), flips(True))
        three = swap(add(p[6 * u : 7 * u], one[:u], two[:u]).astype(p.dtype), "xh")
        return add(p[7 * u :], one[u : 2 * u], two[u:], three)

    previous, current = [None] * CHUNKS, first
    for degree in range(DEGREE):
        following = []
        for k in range(CHUNKS):
            total = scatter(products(order, picks, own, other, gather(current[k])))
            if degree:
                total = 2.0 * total - previous[k].astype(jnp.float32)
            following.append(total.astype(jnp.bfloat16))
        previous, current = current, following

    kept = jnp.concatenate([v[:rows] for v in current], axis=1)
    got = swap(jnp.concatenate([v[rows:] for v in current], axis=1), "c")
    return jnp.where(c == 0, jnp.concatenate([kept, got], axis=1), jnp.concatenate([got, kept], axis=1))


def solution(mesh):
    axes = ("xl", "z", "y", "xh", "c")
    fine = Mesh(mesh.devices.reshape(2, 4, 4, 2, 2), axes)
    row, col = axes[:2], axes[2:]
    placed = (
        P(axes, None),
        P(row, col, None, None, None),
        P(row, col, None),
        P(row, col),
    )
    return jax.shard_map(body, mesh=fine, in_specs=placed, out_specs=P(axes, None), check_vma=False)
```

```python
import functools

import jax
import jax.numpy as jnp
import numpy as np
from jax import lax
from jax.experimental import pallas as pl
from jax.experimental.pallas import tpu as pltpu
from jax.sharding import Mesh, PartitionSpec as P

DEGREE = 3
BLK = 128
CHUNKS = (96, 80, 80)
TURNS = (0, 0, 0, 1, 2, 1, 0, 2, 1, 2, 0, 1, 0, 2, 0, 1, 0, 2, 1, 0, 2, 1, 2, 1, 0, 2, 1, 2, 0, 1, 0, 2, 0, 1, 0, 2, 1, 0, 2, 1, 2, 1, 0, 2, 1, 2, 0, 1, 0, 2, 1, 2, 1, 2)
UNIT = 8


def flips(first):
    return [(2 * i + c, 2 * (i ^ (1 if (c == 0) == first else 3)) + c) for i in range(4) for c in range(2)]


def swap(x, axis):
    return lax.ppermute(x, axis, [(0, 1), (1, 0)])


def product_kernel(order, picks, merged, *refs):
    *pieces, out, held = refs
    step = pl.program_id(0)
    size = held.shape[0] // (8 * UNIT + 1)

    @pl.when(step == 0)
    def _():
        at = 0
        for piece in pieces:
            held[pl.ds(at, piece.shape[0]), :] = piece[...]
            at += piece.shape[0]
        held[pl.ds(at, size), :] = jnp.zeros((size, BLK), held.dtype)

    for half in range(2):
        group = order[2 * step + half]
        for j in range(4):
            a = group * 4 + j
            picked = jnp.concatenate(
                [held[pl.ds(pl.multiple_of(picks[a * 4 + k] * size, 16), size), :] for k in range(4)], axis=1
            )
            total = lax.dot_general(picked, merged[a], (((1,), (1,)), ((), ())), preferred_element_type=jnp.float32)
            at = pl.multiple_of((step * UNIT + half * 4 + j) * size, 16)
            out[pl.ds(at, size), :] = total.astype(out.dtype)


def products(order, picks, merged, pieces):
    rows = sum(piece.shape[0] for piece in pieces)
    whole = pl.BlockSpec(memory_space=pltpu.VMEM)
    return pl.pallas_call(
        product_kernel,
        grid_spec=pltpu.PrefetchScalarGridSpec(
            num_scalar_prefetch=2,
            grid=(8,),
            in_specs=[whole] * (1 + len(pieces)),
            out_specs=whole,
            scratch_shapes=[pltpu.VMEM((rows + rows // (8 * UNIT), BLK), jnp.bfloat16)],
        ),
        out_shape=jax.ShapeDtypeStruct((rows, BLK), jnp.bfloat16),
        compiler_params=pltpu.CompilerParams(vmem_limit_bytes=24 << 20),
        cost_estimate=pl.CostEstimate(flops=2 * rows * 512 * 128, bytes_accessed=4 << 20, transcendentals=0),
        name="products",
    )(order, picks, merged, *pieces)


def add(*terms):
    total = terms[0].astype(jnp.float32)
    for term in terms[1:]:
        total = total + term.astype(jnp.float32)
    return total


def body(start_vectors, tiles, tile_col, tile_count):
    xl, z, y, xh, c = (lax.axis_index(a) for a in ("xl", "z", "y", "xh", "c"))
    rows = start_vectors.shape[0]
    half = start_vectors.shape[1] // 2

    turned = start_vectors.reshape(rows // BLK, BLK, 2 * half).transpose(0, 2, 1)
    mine = lax.dynamic_slice(turned, (0, c * half, 0), (rows // BLK, half, BLK))
    theirs = swap(lax.dynamic_slice(turned, (0, (1 - c) * half, 0), (rows // BLK, half, BLK)), "c")
    both = jnp.concatenate([mine, theirs], axis=0)
    edges = np.cumsum((0,) + CHUNKS)
    first = [both[:, i:j].reshape(-1, BLK) for i, j in zip(edges[:-1], edges[1:])]

    own = tiles[:, 0]
    own, first = lax.optimization_barrier((own, first))
    other = swap(own, "c")
    merged = jnp.concatenate([own[:, 0], own[:, 1], other[:, 0], other[:, 1]], axis=2)

    r, i = tile_col[:, 0] // 4, tile_col[:, 0] % 4
    dx, dz = (r // 4) ^ xl, (r & 3) ^ z
    live = jnp.arange(2, dtype=jnp.int32)[None, :] < tile_count

    def code(core, shift):
        slot = jnp.where(dz == 0, 0, jnp.where(dz == 2, 3, jnp.where(dz == 1 + 2 * core, 1, 2)))
        return jnp.where(live, (slot * 2 + dx) * UNIT + shift + i, 8 * UNIT)

    picks = jnp.concatenate([code(c, 0), swap(code(1 - c, 4), "c")], axis=1).reshape(-1)

    far, near = 3 - 2 * c, 1 + 2 * c
    dy = jnp.stack([far, far, jnp.int32(2), jnp.int32(2), near, near, jnp.int32(0), jnp.int32(0)])
    unit = (y ^ dy) * 2 + (xh ^ np.array([1, 0] * 4, np.int32))
    order = ((unit * 2)[:, None] + (c ^ np.array([[0, 1]], np.int32))).reshape(-1).astype(jnp.int32)

    def chain(v):
        previous = None
        u = v.shape[0]
        for degree in range(DEGREE):
            v = yield v
            pair = jnp.concatenate([v, swap(v, "xl")], axis=0)
            pair = yield pair
            side = lax.ppermute(pair, ("z", "c"), flips(True))
            four = yield jnp.concatenate([pair, side], axis=0)
            rest = lax.ppermute(four, ("z", "c"), flips(False))
            p = yield products(order, picks, merged, (four, rest))
            one = lax.ppermute(p[: 4 * u], ("y", "c"), flips(False))
            sent = yield add(p[4 * u : 6 * u], one[2 * u :]).astype(p.dtype)
            two = lax.ppermute(sent, ("y", "c"), flips(True))
            sent = yield add(p[6 * u : 7 * u], one[:u], two[:u]).astype(p.dtype)
            three = swap(sent, "xh")
            total = add(p[7 * u :], one[u : 2 * u], two[u:], three)
            if degree:
                total = 2.0 * total - previous.astype(jnp.float32)
            previous, v = v, total.astype(v.dtype)
        yield v

    chains = [chain(v) for v in first]
    waiting = [next(steps) for steps in chains]
    last = None
    for k in TURNS:
        if last is None:
            last = waiting[k]
        else:
            last, _ = lax.optimization_barrier((waiting[k], last))
        waiting[k] = chains[k].send(last)

    done = jnp.concatenate([v.reshape(2 * rows // BLK, -1, BLK) for v in waiting], axis=1)
    kept, got = done[: rows // BLK], swap(done[rows // BLK :], "c")
    turned = jnp.where(c == 0, jnp.concatenate([kept, got], axis=1), jnp.concatenate([got, kept], axis=1))
    return turned.transpose(0, 2, 1).reshape(rows, 2 * half)


def solution(mesh):
    axes = ("xl", "z", "y", "xh", "c")
    fine = Mesh(mesh.devices.reshape(2, 4, 4, 2, 2), axes)
    row, col = axes[:2], axes[2:]
    placed = (
        P(axes, None),
        P(row, col, None, None, None),
        P(row, col, None),
        P(row, col),
    )
    return jax.shard_map(body, mesh=fine, in_specs=placed, out_specs=P(axes, None), check_vma=False)
```

```python
import functools

import jax
import jax.numpy as jnp
import numpy as np
from jax import lax
from jax.experimental import pallas as pl
from jax.experimental.pallas import tpu as pltpu
from jax.sharding import Mesh, PartitionSpec as P

DEGREE = 3
BLK = 128
CHUNKS = (64, 64, 64, 64)
TURNS = (0, 1, 0, 1, 0, 2, 3, 1, 2, 0, 3, 2, 1, 3, 0, 2, 0, 1, 3, 0, 1, 2, 0, 1, 3, 2, 1, 0, 3, 2, 1, 3, 0, 2, 1, 3, 2, 0, 3, 1, 2, 0, 3, 1, 0, 2, 1, 0, 3, 2, 1, 0, 3, 2, 1, 3, 2, 0, 3, 2, 1, 3, 0, 2, 1, 3, 1, 0, 2, 3, 2, 3)
UNIT = 8


def flips(first):
    return [(2 * i + c, 2 * (i ^ (1 if (c == 0) == first else 3)) + c) for i in range(4) for c in range(2)]


def swap(x, axis):
    return lax.ppermute(x, axis, [(0, 1), (1, 0)])


def product_kernel(order, picks, own, other, *refs):
    *pieces, out, held = refs
    step = pl.program_id(0)
    size = held.shape[0] // (8 * UNIT + 1)

    @pl.when(step == 0)
    def _():
        at = 0
        for piece in pieces:
            held[pl.ds(at, piece.shape[0]), :] = piece[...]
            at += piece.shape[0]
        held[pl.ds(at, size), :] = jnp.zeros((size, BLK), held.dtype)

    for half in range(2):
        group = order[2 * step + half]
        for j in range(4):
            a = group * 4 + j
            picked = jnp.concatenate(
                [held[pl.ds(pl.multiple_of(picks[a * 4 + k] * size, 16), size), :] for k in range(4)], axis=1
            )
            row = jnp.concatenate([own[a, 0], own[a, 1], other[a, 0], other[a, 1]], axis=1)
            total = lax.dot_general(picked, row, (((1,), (1,)), ((), ())), preferred_element_type=jnp.float32)
            at = pl.multiple_of((step * UNIT + half * 4 + j) * size, 16)
            out[pl.ds(at, size), :] = total.astype(out.dtype)


def products(order, picks, own, other, pieces):
    rows = sum(piece.shape[0] for piece in pieces)
    whole = pl.BlockSpec(memory_space=pltpu.VMEM)
    return pl.pallas_call(
        product_kernel,
        grid_spec=pltpu.PrefetchScalarGridSpec(
            num_scalar_prefetch=2,
            grid=(8,),
            in_specs=[whole] * (2 + len(pieces)),
            out_specs=whole,
            scratch_shapes=[pltpu.VMEM((rows + rows // (8 * UNIT), BLK), jnp.bfloat16)],
        ),
        out_shape=jax.ShapeDtypeStruct((rows, BLK), jnp.bfloat16),
        compiler_params=pltpu.CompilerParams(vmem_limit_bytes=24 << 20),
        cost_estimate=pl.CostEstimate(flops=2 * rows * 512 * 128, bytes_accessed=4 << 20, transcendentals=0),
        name="products",
    )(order, picks, own, other, *pieces)


def add(*terms):
    total = terms[0].astype(jnp.float32)
    for term in terms[1:]:
        total = total + term.astype(jnp.float32)
    return total


def body(start_vectors, tiles, tile_col, tile_count):
    xl, z, y, xh, c = (lax.axis_index(a) for a in ("xl", "z", "y", "xh", "c"))
    rows = start_vectors.shape[0]
    half = start_vectors.shape[1] // 2

    turned = start_vectors.reshape(rows // BLK, BLK, 2 * half).transpose(0, 2, 1)
    mine = lax.dynamic_slice(turned, (0, c * half, 0), (rows // BLK, half, BLK))
    theirs = swap(lax.dynamic_slice(turned, (0, (1 - c) * half, 0), (rows // BLK, half, BLK)), "c")
    both = jnp.concatenate([mine, theirs], axis=0)
    edges = np.cumsum((0,) + CHUNKS)
    first = [both[:, i:j].reshape(-1, BLK) for i, j in zip(edges[:-1], edges[1:])]

    own = tiles[:, 0]
    own, first = lax.optimization_barrier((own, first))
    other = swap(own, "c")

    r, i = tile_col[:, 0] // 4, tile_col[:, 0] % 4
    dx, dz = (r // 4) ^ xl, (r & 3) ^ z
    live = jnp.arange(2, dtype=jnp.int32)[None, :] < tile_count

    def code(core, shift):
        slot = jnp.where(dz == 0, 0, jnp.where(dz == 2, 3, jnp.where(dz == 1 + 2 * core, 1, 2)))
        return jnp.where(live, (slot * 2 + dx) * UNIT + shift + i, 8 * UNIT)

    codes = code(c, 0), swap(code(1 - c, 4), "c")
    picks = jnp.concatenate(codes, axis=1).reshape(-1)
    own, other = (
        jnp.where((at < 8 * UNIT)[:, :, None, None], t, jnp.zeros((), t.dtype)) for at, t in zip(codes, (own, other))
    )

    far, near = 3 - 2 * c, 1 + 2 * c
    dy = jnp.stack([far, far, jnp.int32(2), jnp.int32(2), near, near, jnp.int32(0), jnp.int32(0)])
    unit = (y ^ dy) * 2 + (xh ^ np.array([1, 0] * 4, np.int32))
    order = ((unit * 2)[:, None] + (c ^ np.array([[0, 1]], np.int32))).reshape(-1).astype(jnp.int32)

    def chain(v):
        previous = None
        u = v.shape[0]
        for degree in range(DEGREE):
            v = yield v
            pair = jnp.concatenate([v, swap(v, "xl")], axis=0)
            pair = yield pair
            side = lax.ppermute(pair, ("z", "c"), flips(True))
            four = yield jnp.concatenate([pair, side], axis=0)
            rest = lax.ppermute(four, ("z", "c"), flips(False))
            p = yield products(order, picks, own, other, (four, rest))
            one = lax.ppermute(p[: 4 * u], ("y", "c"), flips(False))
            sent = yield add(p[4 * u : 6 * u], one[2 * u :]).astype(p.dtype)
            two = lax.ppermute(sent, ("y", "c"), flips(True))
            sent = yield add(p[6 * u : 7 * u], one[:u], two[:u]).astype(p.dtype)
            three = swap(sent, "xh")
            total = add(p[7 * u :], one[u : 2 * u], two[u:], three)
            if degree:
                total = 2.0 * total - previous.astype(jnp.float32)
            previous, v = v, total.astype(v.dtype)
        yield v

    chains = [chain(v) for v in first]
    waiting = [next(steps) for steps in chains]
    last = None
    for k in TURNS:
        if last is None:
            last = waiting[k]
        else:
            last, _ = lax.optimization_barrier((waiting[k], last))
        waiting[k] = chains[k].send(last)

    done = jnp.concatenate([v.reshape(2 * rows // BLK, -1, BLK) for v in waiting], axis=1)
    kept, got = done[: rows // BLK], swap(done[rows // BLK :], "c")
    turned = jnp.where(c == 0, jnp.concatenate([kept, got], axis=1), jnp.concatenate([got, kept], axis=1))
    return turned.transpose(0, 2, 1).reshape(rows, 2 * half)


def solution(mesh):
    axes = ("xl", "z", "y", "xh", "c")
    fine = Mesh(mesh.devices.reshape(2, 4, 4, 2, 2), axes)
    row, col = axes[:2], axes[2:]
    placed = (
        P(axes, None),
        P(row, col, None, None, None),
        P(row, col, None),
        P(row, col),
    )
    return jax.shard_map(body, mesh=fine, in_specs=placed, out_specs=P(axes, None), check_vma=False)
```

```python
import functools

import jax
import jax.numpy as jnp
import numpy as np
from jax import lax
from jax.experimental import pallas as pl
from jax.experimental.pallas import tpu as pltpu
from jax.sharding import Mesh, PartitionSpec as P

DEGREE = 3
BLK = 128
CHUNKS = (64, 64, 64, 64)
TURNS = (0, 1, 0, 1, 0, 2, 3, 1, 2, 0, 3, 2, 1, 3, 0, 2, 0, 1, 3, 0, 1, 2, 0, 1, 3, 2, 1, 0, 3, 2, 1, 3, 0, 2, 1, 3, 2, 0, 3, 1, 2, 0, 3, 1, 0, 2, 1, 0, 3, 2, 1, 0, 3, 2, 1, 3, 2, 0, 3, 2, 1, 3, 0, 2, 1, 3, 1, 0, 2, 3, 2, 3)
UNIT = 8


def flips(first):
    return [(2 * i + c, 2 * (i ^ (1 if (c == 0) == first else 3)) + c) for i in range(4) for c in range(2)]


def swap(x, axis):
    return lax.ppermute(x, axis, [(0, 1), (1, 0)])


def product_kernel(order, picks, own, other, *refs):
    *pieces, out, held = refs
    step = pl.program_id(0)
    size = held.shape[0] // (8 * UNIT + 1)

    @pl.when(step == 0)
    def _():
        at = 0
        for piece in pieces:
            held[pl.ds(at, piece.shape[0]), :] = piece[...]
            at += piece.shape[0]
        held[pl.ds(at, size), :] = jnp.zeros((size, BLK), held.dtype)

    for half in range(2):
        group = order[2 * step + half]
        for j in range(4):
            a = group * 4 + j
            picked = jnp.concatenate(
                [held[pl.ds(pl.multiple_of(picks[a * 4 + k] * size, 16), size), :] for k in range(4)], axis=1
            )
            row = jnp.concatenate([own[a, 0], own[a, 1], other[a, 0], other[a, 1]], axis=1)
            total = lax.dot_general(picked, row, (((1,), (1,)), ((), ())), preferred_element_type=jnp.float32)
            at = pl.multiple_of((step * UNIT + half * 4 + j) * size, 16)
            out[pl.ds(at, size), :] = total.astype(out.dtype)


def products(order, picks, own, other, pieces):
    rows = sum(piece.shape[0] for piece in pieces)
    whole = pl.BlockSpec(memory_space=pltpu.VMEM)
    return pl.pallas_call(
        product_kernel,
        grid_spec=pltpu.PrefetchScalarGridSpec(
            num_scalar_prefetch=2,
            grid=(8,),
            in_specs=[whole] * (2 + len(pieces)),
            out_specs=whole,
            scratch_shapes=[pltpu.VMEM((rows + rows // (8 * UNIT), BLK), jnp.bfloat16)],
        ),
        out_shape=jax.ShapeDtypeStruct((rows, BLK), jnp.bfloat16),
        compiler_params=pltpu.CompilerParams(vmem_limit_bytes=24 << 20),
        cost_estimate=pl.CostEstimate(flops=2 * rows * 512 * 128, bytes_accessed=4 << 20, transcendentals=0),
        name="products",
    )(order, picks, own, other, *pieces)


def add(*terms):
    total = terms[0].astype(jnp.float32)
    for term in terms[1:]:
        total = total + term.astype(jnp.float32)
    return total


def body(start_vectors, tiles, tile_col, tile_count):
    xl, z, y, xh, c = (lax.axis_index(a) for a in ("xl", "z", "y", "xh", "c"))
    rows = start_vectors.shape[0]
    half = start_vectors.shape[1] // 2

    turned = start_vectors.reshape(rows // BLK, BLK, 2 * half).transpose(0, 2, 1)
    mine = lax.dynamic_slice(turned, (0, c * half, 0), (rows // BLK, half, BLK))
    theirs = swap(lax.dynamic_slice(turned, (0, (1 - c) * half, 0), (rows // BLK, half, BLK)), "c")
    both = jnp.concatenate([mine, theirs], axis=0)
    edges = np.cumsum((0,) + CHUNKS)
    first = [both[:, i:j].reshape(-1, BLK) for i, j in zip(edges[:-1], edges[1:])]

    own = tiles[:, 0]
    own, first = lax.optimization_barrier((own, first))
    other = swap(own, "c")

    def prepare(tile_col, tile_count, y, xh, c, own, other):
        r, i = tile_col[:, 0] // 4, tile_col[:, 0] % 4
        dx, dz = (r // 4) ^ xl, (r & 3) ^ z
        live = jnp.arange(2, dtype=jnp.int32)[None, :] < tile_count

        def code(core, shift):
            slot = jnp.where(dz == 0, 0, jnp.where(dz == 2, 3, jnp.where(dz == 1 + 2 * core, 1, 2)))
            return jnp.where(live, (slot * 2 + dx) * UNIT + shift + i, 8 * UNIT)

        codes = code(c, 0), swap(code(1 - c, 4), "c")
        picks = jnp.concatenate(codes, axis=1).reshape(-1)
        own, other = (
            jnp.where((at < 8 * UNIT)[:, :, None, None], t, jnp.zeros((), t.dtype)) for at, t in zip(codes, (own, other))
        )

        far, near = 3 - 2 * c, 1 + 2 * c
        dy = jnp.stack([far, far, jnp.int32(2), jnp.int32(2), near, near, jnp.int32(0), jnp.int32(0)])
        unit = (y ^ dy) * 2 + (xh ^ np.array([1, 0] * 4, np.int32))
        order = ((unit * 2)[:, None] + (c ^ np.array([[0, 1]], np.int32))).reshape(-1).astype(jnp.int32)
        return order, picks, own, other

    def chain(v):
        previous = None
        u = v.shape[0]
        for degree in range(DEGREE):
            v = yield v
            pair = jnp.concatenate([v, swap(v, "xl")], axis=0)
            pair = yield pair
            side = lax.ppermute(pair, ("z", "c"), flips(True))
            four = yield jnp.concatenate([pair, side], axis=0)
            rest = lax.ppermute(four, ("z", "c"), flips(False))
            p = yield products(*prepared, (four, rest))
            one = lax.ppermute(p[: 4 * u], ("y", "c"), flips(False))
            sent = yield add(p[4 * u : 6 * u], one[2 * u :]).astype(p.dtype)
            two = lax.ppermute(sent, ("y", "c"), flips(True))
            sent = yield add(p[6 * u : 7 * u], one[:u], two[:u]).astype(p.dtype)
            three = swap(sent, "xh")
            total = add(p[7 * u :], one[u : 2 * u], two[u:], three)
            if degree:
                total = 2.0 * total - previous.astype(jnp.float32)
            previous, v = v, total.astype(v.dtype)
        yield v

    chains = [chain(v) for v in first]
    waiting = [next(steps) for steps in chains]
    last, prepared = None, []
    for turn, k in enumerate(TURNS):
        if last is None:
            last = waiting[k]
        else:
            last, _ = lax.optimization_barrier((waiting[k], last))
        if turn == 2:
            tied = lax.optimization_barrier((tile_col, tile_count, y, xh, c, last))
            prepared = prepare(*tied[:5], own, other)
        waiting[k] = chains[k].send(last)

    done = [v.reshape(2 * rows // BLK, -1, BLK) for v in waiting]
    kept = jnp.concatenate([v[: rows // BLK] for v in done], axis=1)
    got = jnp.concatenate([swap(v[rows // BLK :], "c") for v in done], axis=1)
    turned = jnp.where(c == 0, jnp.concatenate([kept, got], axis=1), jnp.concatenate([got, kept], axis=1))
    return turned.transpose(0, 2, 1).reshape(rows, 2 * half)


def solution(mesh):
    axes = ("xl", "z", "y", "xh", "c")
    fine = Mesh(mesh.devices.reshape(2, 4, 4, 2, 2), axes)
    row, col = axes[:2], axes[2:]
    placed = (
        P(axes, None),
        P(row, col, None, None, None),
        P(row, col, None),
        P(row, col),
    )
    return jax.shard_map(body, mesh=fine, in_specs=placed, out_specs=P(axes, None), check_vma=False)
```
